512 devices in a mesh: grid: 64 (over y, z_hi, core), tm: 8 (over z_lo, x).
Axes of the slice: x: 4, y: 8, z: 8 (z_hi: 4, z_lo: 2; z = z_hi * 2 + z_lo), core: 2. Of those that a mesh axis runs over, the one named last changes fastest.
Arguments:
- observations: float32 [32, 32, 64, 768], P('tm', None, 'grid'), may hold values from -40 to 40
- a_factor: float32 [64, 256], P('grid'), may hold values from -5 to 5
- b_factor: float32 [768, 128], replicated, may hold values from -5 to 5
- c_factor: float32 [32, 16], replicated, may hold values from -5 to 5
- e_factor: float32 [32, 8], P('tm'), may hold values from -5 to 5
- core: float32 [8, 16, 128, 256], P(None, None, 'grid'), may hold values from -5 to 5
Outputs:
- residual: float32 [32, 32, 64, 768], P('tm', None, 'grid')
- a_new: float32 [64, 256], P('grid')
- b_new: float32 [768, 128], replicated
- c_new: float32 [32, 16], replicated
- e_new: float32 [32, 8], P('tm')
- core_new: float32 [8, 16, 128, 256], P(None, None, 'grid')
The draws below stay inside these ranges and needn't reach their ends.
All inputs are finite; a program needn't handle non-finite values.
Results may differ from the reference program's by a relative error of at most 0.0003.
Values sent between devices are 32-bit elements; how exact they have to be, the bound alone decides.
No kernel may reach another device: no remote copies, remote signals or barrier semaphores. Data moves between devices by JAX's collectives and lax.ppermute only.
A program may use at most 64 MiB of HBM per device.

```python
import jax
import jax.numpy as jnp
from jax import lax

RA = 256
RB = 128
RC = 16
RD = 8
LEV = 32
STEPS = 2
LAT = 768
LON = 64
HOURS = 32


def draw_observations(key, part):
    key = jax.random.fold_in(key, 11)
    key_base, key_lat = jax.random.split(key)
    lon_scale = 10.0 ** (jnp.arange(LON, dtype=jnp.float32) / LON - 0.5)
    lat_scale = 10.0 ** (jax.random.uniform(key_lat, (LAT,), jnp.float32) - 0.5)
    shape = (HOURS, LEV, LON, LAT)
    base = jax.random.truncated_normal(key_base, -4.0, 4.0, shape, jnp.float32)
    return (base * lon_scale[None, None, :, None] * lat_scale[None, None, None, :]).astype(jnp.float32)


def shard_levels(own_key, dims, shards, least, high):
    factor_of, own = 1.0, jax.random.fold_in(own_key, 6)
    for axis_at, blocks in shards:
        heights = jnp.exp(jax.random.uniform(jax.random.fold_in(own, axis_at), (blocks,), jnp.float32, least / len(shards), high / len(shards)))
        factor_of = factor_of * jnp.repeat(heights, dims[axis_at] // blocks).reshape([-1 if axis == axis_at else 1 for axis in range(len(dims))])
    return factor_of


def centred(own_key, extent, scale, limit, shards=(), kind=jnp.bfloat16):
    loudness = shard_levels(own_key, extent, shards, -0.22, 0.18) if shards else 1.0
    result = jax.random.normal(own_key, extent, jnp.float32) * scale * loudness
    return jnp.minimum(jnp.maximum(result, -limit), limit).astype(kind)


def setup_inputs(seed: int = 0) -> dict:
    key_list = jax.random.split(jax.random.key(seed), 7)
    return {
        "observations": draw_observations(jax.random.fold_in(key_list[6], 71), 0),
        "a_factor": centred(key_list[1], (LON, RA), 1.0, 5.0, ((0, 64),), jnp.float32),
        "b_factor": centred(key_list[2], (LAT, RB), 1.0, 5.0, (), jnp.float32),
        "c_factor": centred(key_list[3], (LEV, RC), 1.0, 5.0, (), jnp.float32),
        "e_factor": centred(key_list[4], (HOURS, RD), 1.0, 5.0, ((0, 8),), jnp.float32),
        "core": centred(key_list[5], (RD, RC, RB, RA), 1.0, 5.0, ((2, 64),), jnp.float32),
    }


ETA = 0.2
EPS = 1e-06

def core_product(form, *operands):
    return jnp.einsum(form, *operands, precision=lax.Precision.HIGHEST)

def advance(param, grad):
    return param - ETA * grad / jnp.sqrt(jnp.mean(grad * grad) + EPS)

def gradients(a_fac, level_factor_matrix, c_fac, e_fac, core, observations, step_scale):

    def visit(carry, pair):
        hourly_slice, e_row = pair
        kern = core_product('dcba,d->cba', core, e_row)
        near = core_product('cba,la->cbl', kern, a_fac)
        full_tensor = core_product('cbl,vc->vbl', near, c_fac)
        fit_residual = step_scale * core_product('jme,am->jea', full_tensor, level_factor_matrix) - hourly_slice
        level_factor_gradient = step_scale * core_product('akz,aok->zo', fit_residual, full_tensor)
        upward_levels = step_scale * core_product('nae,ed->nda', fit_residual, level_factor_matrix)
        grad_c = core_product('vbl,cbl->vc', upward_levels, near)
        urank = core_product('vbl,vc->cbl', upward_levels, c_fac)
        grad_a = core_product('cbl,cba->la', urank, kern)
        vrank = core_product('cbl,la->cba', urank, a_fac)
        grad_e = core_product('cba,dcba->d', vrank, core)
        grad_g = core_product('cba,d->dcba', vrank, e_row)
        acc_a, acc_b, acc_c, acc_g = carry
        return ((acc_a + grad_a, acc_b + level_factor_gradient, acc_c + grad_c, acc_g + grad_g), grad_e)
    start = (jnp.zeros(a_fac.shape, jnp.float32), jnp.zeros(level_factor_matrix.shape, jnp.float32), jnp.zeros(c_fac.shape, jnp.float32), jnp.zeros(core.shape, jnp.float32))
    sums, grad_e = lax.scan(visit, start, (observations, e_fac))
    return (sums[0], sums[1], sums[2], grad_e, sums[3])

def reference(observations, a_factor, b_factor, c_factor, e_factor, core):
    step_scale = float(RA * RB * RC * RD) ** (-0.5)
    params = (a_factor, b_factor, c_factor, e_factor, core)
    for step in range(STEPS):
        grads = gradients(*params, observations, step_scale)
        params = tuple((advance(p, g) for p, g in zip(params, grads)))
    a_fac, level_factor_matrix, c_fac, e_fac, core_fac = params

    def model_hour(pair):
        hourly_slice, e_row = pair
        kern = core_product('dcba,d->cba', core_fac, e_row)
        near = core_product('cba,la->cbl', kern, a_fac)
        full_tensor = core_product('cbl,vc->vbl', near, c_fac)
        return step_scale * core_product('jme,am->jea', full_tensor, level_factor_matrix) - hourly_slice
    residual = lax.map(model_hour, (observations, e_fac))
    return (residual, a_fac, level_factor_matrix, c_fac, e_fac, core_fac)
```

```python
import jax
import jax.numpy as jnp
from jax import lax
from jax.sharding import Mesh, PartitionSpec as P

STEPS = 2
ETA = 0.2
EPS = 1e-06

FAR = ("y", "zh")
NEAR = ("zl", "x", "co")
NF, NN = 32, 16


def dot(form, *ops):
    return jnp.einsum(form, *ops, precision=lax.Precision.HIGHEST)


def swap(x, axes):
    return lax.all_to_all(x, axes, 0, 0, tiled=True)


def spread(x, n, axes):
    return swap(jnp.broadcast_to(x[None], (n,) + x.shape), axes)


def rows(n, *parts):
    x = jnp.concatenate(parts, axis=1)
    return jnp.pad(x, ((0, 0), (0, n - x.shape[1]), (0, 0)))


def rate(total, count):
    return ETA / jnp.sqrt(total / count + EPS)


def model_products(a_two, core_part):
    return dot("cba,la->lcb", core_part, a_two)


def kron(e_t, c_t):
    x = e_t[:, None, :, None] * c_t[None, :, None, :]
    return x.reshape(e_t.shape[0] * c_t.shape[0], e_t.shape[1] * c_t.shape[1])


def shards(observations, a_factor, b_factor, c_factor, e_factor, core):
    scale = float(256 * 128 * 16 * 8) ** (-0.5)
    tm = lax.axis_index("zl") * 4 + lax.axis_index("x")
    co = lax.axis_index("co")
    far = lax.axis_index("y") * 4 + lax.axis_index("zh")
    near = tm * 2 + co

    own = lax.dynamic_slice_in_dim(core, tm, 1, 0).reshape(2, 8, 4, 128)
    first = rows(40, own.reshape(2, 32, 128), jnp.broadcast_to(a_factor.reshape(1, 2, 128), (2, 2, 128)))
    first = swap(first, "co")
    g_mine = first[:, :32].reshape(2, 8, 2, 256).transpose(1, 0, 2, 3)
    a_two = first[:, 32:34].reshape(2, 256)
    second = jnp.concatenate([g_mine.reshape(64, 128), a_two.reshape(4, 128), jnp.zeros((4, 128))])
    second = spread(second, NF, FAR)
    core_part = second[:, :64].reshape(NF, 8, 4, 256).transpose(1, 0, 2, 3).reshape(8, 128, 256)
    a_all = second[:, 64:68].reshape(64, 256)

    obs_t = observations.reshape(128, NN, 48).transpose(1, 2, 0)
    products = model_products(a_two, core_part)
    e_row = jnp.pad(e_factor.reshape(1, 32), ((0, 0), (0, 96)))
    third = rows(
        72,
        obs_t,
        jnp.broadcast_to(products.reshape(1, 16, 128), (NN, 16, 128)),
        jnp.broadcast_to(e_row[None], (NN, 1, 128)),
    )
    third = swap(third, NEAR)
    obs_part = third[:, :48].reshape(8, 2, 48, 128).transpose(1, 2, 0, 3).reshape(2, 48, 1024)
    e_t = third[::2, 64, :32].reshape(32, 8).T
    prods = third[:, 48:64].reshape(NN, 2, 8, 128)
    b_part = lax.dynamic_slice_in_dim(b_factor, near * 48, 48, 0)
    c_t = c_factor.T

    for step in range(STEPS):
        last = step == STEPS - 1
        w = prods.transpose(1, 0, 2, 3).reshape(2, 128, 128)
        ec = kron(e_t, c_t)
        q = dot("lkb,kn->lbn", w, ec)
        res = scale * dot("tb,lbn->ltn", b_part, q) - obs_part
        gb_part = scale * dot("ltn,lbn->tb", res, q)
        up = scale * dot("tb,ltn->lbn", b_part, res)
        p_part = dot("kn,lbn->lkb", ec, up)
        x = dot("lkb,lbn->kn", w, up).reshape(8, 16, 32, 32)
        ge_t = dot("dchv,cv->dh", x, c_t)
        gc_t = dot("dchv,dh->cv", x, e_t)
        gec = jnp.concatenate([gc_t, jnp.pad(ge_t, ((0, 8), (0, 0))), jnp.zeros((16, 64))], axis=1)

        x1 = rows(24, p_part.reshape(2, NN, 8, 128).transpose(1, 0, 2, 3).reshape(NN, 16, 128), gec[:, None, :])
        x1 = jnp.sum(swap(x1, NEAR), axis=0)
        p_two = x1[:16]
        ga_part = dot("lcb,cba->la", p_two.reshape(2, 8, 128), core_part)

        x2 = rows(
            24,
            jnp.broadcast_to(p_two[None], (NF, 16, 128)),
            jnp.pad(gb_part, ((0, 16), (0, 0))).reshape(NF, 2, 128),
            jnp.broadcast_to(x1[None, 16:17], (NF, 1, 128)),
        )
        x2 = swap(x2, FAR)
        p_all = x2[:, :16].reshape(64, 8, 128)
        g_core = dot("lcb,la->cba", p_all, a_all)
        x2s = jnp.sum(x2[:, 16:19], axis=0)
        gb_rows, gec_row = x2s[:2], x2s[2:3]

        scal = jnp.stack([jnp.sum(g_core * g_core), jnp.sum(gb_rows * gb_rows)])
        x3 = jnp.concatenate([ga_part.reshape(4, 128), gec_row, jnp.pad(scal[None], ((0, 0), (0, 126))), jnp.zeros((2, 128))])
        x3 = spread(x3, NN, NEAR)
        ga_two = jnp.sum(x3[:, :4], axis=0)
        scal = jnp.sum(x3[:, 5, :2], axis=0)
        gc_t = x3[:, 4, :32]
        ge_t = x3[:8, 4, 32:64]
        core_part = core_part - rate(scal[0], 4194304) * g_core
        c_t = c_t - rate(jnp.sum(gc_t * gc_t), 512) * gc_t
        e_t = e_t - rate(jnp.sum(ge_t * ge_t), 256) * ge_t

        x4 = jnp.concatenate([ga_two, gb_rows, jnp.broadcast_to(scal[1:2, None], (1, 128)), jnp.zeros((1, 128))])
        x4 = spread(x4, NF, FAR)
        ga_all = x4[:, :4].reshape(64, 256)
        gb_part = x4[:, 4:6].reshape(64, 128)[:48]
        a_all = a_all - rate(jnp.sum(ga_all * ga_all), 16384) * ga_all
        b_part = b_part - rate(jnp.sum(x4[:, 6, 0]), 98304) * gb_part
        a_two = lax.dynamic_slice_in_dim(a_all, far * 2, 2, 0)

        products = model_products(a_two, core_part).reshape(16, 128)
        if not last:
            prods = spread(products, NN, NEAR).reshape(NN, 2, 8, 128)

    mine = lax.dynamic_slice_in_dim(core_part, far * 4, 4, 1).reshape(8, 2, 2, 256)
    mine = mine.transpose(1, 0, 2, 3).reshape(1, 2, 32, 128)
    mine = jnp.broadcast_to(mine, (8, 2, 32, 128)).reshape(NN, 32, 128)
    x5 = rows(
        96,
        jnp.broadcast_to(products[None], (NN, 16, 128)),
        jnp.broadcast_to(b_part[None], (NN, 48, 128)),
        mine,
    )
    x5 = swap(x5, NEAR)
    b_new = x5[:, 16:64].reshape(768, 128)
    core_new = x5[:, 64:].reshape(8, 16, 2, 256)
    w = lax.dynamic_index_in_dim(x5[:, :16].reshape(NN, 2, 8, 128), co, 1, False).reshape(128, 128)
    e_own = lax.dynamic_slice_in_dim(e_t, tm * 4, 4, 1)
    q = dot("kn,kb->nb", kron(e_own, c_t), w)
    residual = scale * dot("nb,tb->nt", q, b_new) - observations.reshape(128, 768)
    a_new = lax.dynamic_slice_in_dim(a_two, co, 1, 0)
    return (residual.reshape(4, 32, 1, 768), a_new, b_new, c_t.T, e_own.T, core_new)


def solution(mesh):
    fine = Mesh(mesh.devices.reshape(8, 4, 2, 2, 4), ("y", "zh", "co", "zl", "x"))
    grid, tm = ("y", "zh", "co"), ("zl", "x")
    specs = (P(tm, None, grid, None), P(grid, None), P(), P(), P(tm, None), P(None, None, grid, None))
    return jax.shard_map(shards, mesh=fine, in_specs=specs, out_specs=specs, check_vma=False)
```

```python
import functools

import jax
import jax.numpy as jnp
from jax import lax
from jax.experimental import pallas as pl
from jax.experimental.pallas import tpu as pltpu
from jax.sharding import Mesh, PartitionSpec as P

STEPS = 2
ETA = 0.2
EPS = 1e-06
SCALE = float(256 * 128 * 16 * 8) ** (-0.5)

FAR = ("y", "zh")
NEAR = ("zl", "x", "co")
NF, NN = 32, 16
HIGH, FULL = lax.Precision.HIGH, lax.Precision.HIGHEST
f32 = jnp.float32


def swap(x, axes):
    return lax.all_to_all(x, axes, 0, 0, tiled=True)


def dg(a, b, ca, cb, precision=HIGH):
    return lax.dot_general(a, b, (((ca,), (cb,)), ((), ())), precision=precision, preferred_element_type=f32)


def rate(total, count):
    return ETA * lax.rsqrt(total / count + EPS)


def call(body, outs, *ins, smem=0):
    specs = [pl.BlockSpec(memory_space=pltpu.SMEM)] * smem + [pl.BlockSpec(memory_space=pltpu.VMEM)] * (len(ins) - smem)
    return pl.pallas_call(
        body,
        out_shape=[jax.ShapeDtypeStruct(s, f32) for s in outs],
        in_specs=specs,
        out_specs=[pl.BlockSpec(memory_space=pltpu.VMEM)] * len(outs),
        compiler_params=pltpu.CompilerParams(vmem_limit_bytes=32 * 1024 * 1024),
    )(*ins)


def chosen(rows, lanes, kind, start=0):
    r = lax.broadcasted_iota(jnp.int32, (rows, lanes), 0)
    n = lax.broadcasted_iota(jnp.int32, (rows, lanes), 1)
    n = n // 32 + start if kind == "h" else n % 32
    return jnp.where(r == n, 1.0, 0.0).astype(f32)


def expanded(ec_t, lanes, start=0):
    ce = dg(ec_t[:, :32], chosen(32, lanes, "v"), 1, 0, FULL)
    ee = dg(ec_t[:8, 32:64], chosen(32, lanes, "h", start), 1, 0, FULL)
    return ee, ce, (ee[:, None, :] * ce[None, :, :]).reshape(128, lanes)


def residual_body(first, *refs):
    if first:
        third_ref, c_ref, b_ref, x1_ref, gb_ref, obs_ref, ec_ref = refs
        for l in range(2):
            for t in range(8):
                obs_ref[l, :, 128 * t : 128 * t + 128] = third_ref[2 * t + l, :48, :]
        ec_t = c_ref[...]
        e_sum = third_ref[0, 64:72, :]
        for t in range(1, 8):
            e_sum = e_sum + third_ref[2 * t, 64:72, :]
        ec_t = ec_t + jnp.concatenate([e_sum, jnp.zeros_like(e_sum)], axis=0)
        ec_ref[...] = ec_t
        w = [third_ref[:, 48 + 8 * l : 56 + 8 * l, :].reshape(128, 128) for l in range(2)]
    else:
        w_ref, ec_ref, b_ref, obs_ref, x1_ref, gb_ref = refs
        ec_t = ec_ref[...]
        w = [w_ref[:, 8 * l : 8 * l + 8, :].reshape(128, 128) for l in range(2)]
    ee, ce, ec = expanded(ec_t, 1024)
    b = b_ref[...]
    bt = b.T
    gb, x = None, None
    x1_ref[:, 16:24, :] = jnp.zeros((16, 8, 128), f32)
    for l in range(2):
        q = dg(w[l].T, ec, 1, 0)
        res = SCALE * dg(b, q, 1, 0) - obs_ref[l]
        gb_l = dg(res, q, 1, 1)
        gb = gb_l if gb is None else gb + gb_l
        up = SCALE * dg(bt, res, 1, 0)
        x1_ref[:, 8 * l : 8 * l + 8, :] = dg(ec, up, 1, 1).reshape(16, 8, 128)
        x_l = dg(w[l], up, 1, 0)
        x = x_l if x is None else x + x_l
    gb_ref[...] = SCALE * gb
    x = x.reshape(8, 16, 1024)
    ge = dg(jnp.sum(x * ce[None], axis=1), chosen(32, 1024, "h"), 1, 1, FULL)
    gc = dg(jnp.sum(x * ee[:, None], axis=0), chosen(32, 1024, "v"), 1, 1, FULL)
    for r in range(16):
        x1_ref[r, 16:17, 0:32] = gc[r : r + 1]
        if r < 8:
            x1_ref[r, 16:17, 32:64] = ge[r : r + 1]


def near_sum_body(x1_ref, gb_ref, core_ref, x2_ref, ga_ref):
    s = jnp.sum(x1_ref[...], axis=0)
    acc = None
    for c in range(8):
        p = jnp.concatenate([s[c : c + 1], s[8 + c : 9 + c]], axis=0)
        t = dg(p, core_ref[c], 1, 0)
        acc = t if acc is None else acc + t
    ga_ref[...] = jnp.concatenate([acc[:, :128], acc[:, 128:], jnp.zeros((4, 128), f32)], axis=0)
    tail = jnp.concatenate([jnp.zeros((2, 128), f32), s[16:17], jnp.zeros((5, 128), f32)], axis=0)
    x2_ref[...] = jnp.broadcast_to(jnp.concatenate([s[:16], tail], axis=0)[None], (32, 24, 128))
    for k in range(24):
        x2_ref[k, 16:18, :] = gb_ref[2 * k : 2 * k + 2, :]


def core_grad_body(x2_ref, a_ref, ga_ref, x3_ref, g_ref, gb_ref):
    a = a_ref[...]
    sq = jnp.zeros((1, 128), f32)
    for c in range(8):
        p = jnp.concatenate([x2_ref[:, c, :], x2_ref[:, 8 + c, :]], axis=0)
        g = dg(p.T, a, 1, 0)
        g_ref[c] = g
        s = jnp.sum(g * g, axis=0, keepdims=True)
        sq = sq + s[:, :128] + s[:, 128:]
    s = jnp.sum(x2_ref[:, 16:24, :], axis=0)
    gb_ref[...] = s
    gb = s[0:2]
    rows = jnp.concatenate(
        [ga_ref[0:4], s[2:3], sq, jnp.sum(gb * gb, axis=0, keepdims=True), jnp.zeros((1, 128), f32)], axis=0
    )
    x3_ref[...] = jnp.broadcast_to(rows[None], (16, 8, 128))


def near_update_body(x3_ref, gb_ref, ec_ref, x4_ref, new_ref, sq_ref):
    s = jnp.sum(x3_ref[...], axis=0)
    g = x3_ref[:, 4, :]
    lane = lax.broadcasted_iota(jnp.int32, (16, 128), 1)
    gc = jnp.where(lane < 32, g, 0.0)
    ge = jnp.where(jnp.logical_and(lane >= 32, lane < 64), g, 0.0)
    new_ref[...] = ec_ref[...] - rate(jnp.sum(gc * gc), 512.0) * gc - rate(jnp.sum(ge * ge), 256.0) * ge
    sq_ref[...] = jnp.broadcast_to(jnp.sum(s[5:6], axis=1, keepdims=True), (8, 128))
    rows = jnp.concatenate([s[0:4], gb_ref[0:2], s[6:7], jnp.zeros((1, 128), f32)], axis=0)
    x4_ref[...] = jnp.broadcast_to(rows[None], (32, 8, 128))


def far_update_body(far_ref, x4_ref, a_ref, b_ref, core_ref, g_ref, sq_ref, x5_ref, a_new, b_new, core_new):
    ga = jnp.concatenate(
        [
            jnp.concatenate([x4_ref[:, 0, :], x4_ref[:, 1, :]], axis=0),
            jnp.concatenate([x4_ref[:, 2, :], x4_ref[:, 3, :]], axis=0),
        ],
        axis=1,
    )
    a_new[...] = a_ref[...] - rate(jnp.sum(ga * ga), 16384.0) * ga
    sb = jnp.sum(x4_ref[:, 6, :])
    rb = rate(sb, 98304.0)
    for k in range(24):
        b_new[2 * k : 2 * k + 2, :] = b_ref[2 * k : 2 * k + 2, :] - rb * x4_ref[k, 4:6, :]
    far = far_ref[0]
    a_two = jnp.concatenate([a_new[pl.ds(far, 1), :], a_new[pl.ds(far + 32, 1), :]], axis=0)
    rg = ETA * lax.rsqrt(sq_ref[0:1, 0:1] * (1.0 / 4194304) + EPS)
    top, low = [], []
    for c in range(8):
        g = core_ref[c] - rg * g_ref[c]
        core_new[c] = g
        w = dg(a_two, g, 1, 1)
        top.append(w[0:1])
        low.append(w[1:2])
    x5_ref[...] = jnp.broadcast_to(jnp.concatenate(top + low, axis=0)[None], (16, 16, 128))


def first_products_body(core_ref, a_ref, x_ref):
    top, low = [], []
    for c in range(8):
        w = dg(a_ref[...], core_ref[c], 1, 1)
        top.append(w[0:1])
        low.append(w[1:2])
    x_ref[...] = jnp.concatenate(top + low, axis=0)


def final_body(idx_ref, x5_ref, ec_ref, obs_ref, res_ref, b_ref):
    tm, co = idx_ref[0], idx_ref[1]
    _, _, ec = expanded(ec_ref[...], 128, 4 * tm)
    w = x5_ref[:, pl.ds(pl.multiple_of(co * 8, 8), 8), :].reshape(128, 128)
    b = x5_ref[:, 16:64, :].reshape(768, 128)
    b_ref[...] = b
    q = dg(ec.T, w, 1, 0)
    res_ref[...] = SCALE * dg(q, b, 1, 1) - obs_ref[...]


def shards(observations, a_factor, b_factor, c_factor, e_factor, core):
    tm = lax.axis_index("zl") * 4 + lax.axis_index("x")
    co = lax.axis_index("co")
    far = lax.axis_index("y") * 4 + lax.axis_index("zh")
    near = tm * 2 + co
    far_i = far.astype(jnp.int32).reshape(1)

    own = lax.dynamic_slice_in_dim(core, tm, 1, 0).reshape(2, 32, 128)
    a_own = jnp.pad(a_factor.reshape(1, 2, 128), ((0, 0), (0, 6), (0, 0)))
    first = jnp.concatenate([own, jnp.broadcast_to(a_own, (2, 8, 128))], axis=1)
    first = swap(first, "co")
    g_mine = first[:, :32].reshape(2, 8, 2, 256).transpose(1, 0, 2, 3)
    a_two = first[:, 32:34].reshape(2, 256)
    second = jnp.concatenate([g_mine.reshape(64, 128), a_two.reshape(4, 128), jnp.zeros((4, 128), f32)])
    second = swap(jnp.broadcast_to(second[None], (NF, 72, 128)), FAR)
    core_part = second[:, :64].reshape(NF, 8, 4, 256).transpose(1, 0, 2, 3).reshape(8, 128, 256)
    a_all = second[:, 64:68].reshape(NF, 2, 256).transpose(1, 0, 2).reshape(64, 256)

    obs_t = observations.reshape(128, NN, 48).transpose(1, 2, 0)
    (products,) = call(first_products_body, [(16, 128)], core_part, a_two)
    e_own = lax.dynamic_update_slice(jnp.zeros((8, 128), f32), e_factor.T, (0, 32 + 4 * tm))
    rest = jnp.concatenate([products, e_own])
    third = jnp.concatenate([obs_t, jnp.broadcast_to(rest[None], (NN, 24, 128))], axis=1)
    third = swap(third, NEAR)
    b_part = lax.dynamic_slice_in_dim(b_factor, near * 48, 48, 0)
    c_t = jnp.pad(c_factor.T, ((0, 0), (0, 96)))

    for step in range(STEPS):
        if step == 0:
            x1, gb, obs_part, ec_t = call(
                functools.partial(residual_body, True),
                [(16, 24, 128), (48, 128), (2, 48, 1024), (16, 128)],
                third, c_t, b_part,
            )
        else:
            x1, gb = call(
                functools.partial(residual_body, False), [(16, 24, 128), (48, 128)], x5, ec_t, b_part, obs_part
            )
        x2, ga = call(near_sum_body, [(32, 24, 128), (8, 128)], swap(x1, NEAR), gb, core_part)
        x3, g_core, gb = call(core_grad_body, [(16, 8, 128), (8, 128, 256), (8, 128)], swap(x2, FAR), a_all, ga)
        x4, ec_t, sq = call(near_update_body, [(32, 8, 128), (16, 128), (8, 128)], swap(x3, NEAR), gb, ec_t)
        x5, a_all, b_part, core_part = call(
            far_update_body,
            [(16, 16, 128), (64, 256), (48, 128), (8, 128, 256)],
            far_i, swap(x4, FAR), a_all, b_part, core_part, g_core, sq,
            smem=1,
        )
        if step < STEPS - 1:
            x5 = swap(x5, NEAR)

    mine = lax.dynamic_slice_in_dim(core_part, far * 4, 4, 1).reshape(8, 2, 2, 256)
    mine = mine.transpose(1, 0, 2, 3).reshape(1, 2, 32, 128)
    mine = jnp.broadcast_to(mine, (8, 2, 32, 128)).reshape(NN, 32, 128)
    x5 = swap(jnp.concatenate([x5, jnp.broadcast_to(b_part[None], (NN, 48, 128)), mine], axis=1), NEAR)
    core_new = x5[:, 64:].reshape(8, 16, 2, 256)
    idx = jnp.stack([tm, co]).astype(jnp.int32)
    residual, b_new = call(
        final_body, [(128, 768), (768, 128)], idx, x5, ec_t, observations.reshape(128, 768), smem=1
    )
    a_new = lax.dynamic_slice_in_dim(a_all, co * 32 + far, 1, 0)
    e_new = lax.dynamic_slice(ec_t, (0, 32 + 4 * tm), (8, 4)).T
    return (residual.reshape(4, 32, 1, 768), a_new, b_new, ec_t[:, :32].T, e_new, core_new)


def solution(mesh):
    fine = Mesh(mesh.devices.reshape(8, 4, 2, 2, 4), ("y", "zh", "co", "zl", "x"))
    grid, tm = ("y", "zh", "co"), ("zl", "x")
    specs = (P(tm, None, grid, None), P(grid, None), P(), P(), P(tm, None), P(None, None, grid, None))
    return jax.shard_map(shards, mesh=fine, in_specs=specs, out_specs=specs, check_vma=False)
```

```python
import functools

import jax
import jax.numpy as jnp
from jax import lax
from jax.experimental import pallas as pl
from jax.experimental.pallas import tpu as pltpu
from jax.sharding import Mesh, PartitionSpec as P

STEPS = 2
ETA = 0.2
EPS = 1e-06
SCALE = float(256 * 128 * 16 * 8) ** (-0.5)

FAR = ("y", "zh")
NEAR = ("zl", "x", "co")
NF, NN = 32, 16
HIGH, FULL = lax.Precision.HIGH, lax.Precision.HIGHEST
f32 = jnp.float32


def swap(x, axes):
    return lax.all_to_all(x, axes, 0, 0, tiled=True)


def dg(a, b, ca, cb, precision=HIGH):
    return lax.dot_general(a, b, (((ca,), (cb,)), ((), ())), precision=precision, preferred_element_type=f32)


def rate(total, count):
    return ETA * lax.rsqrt(total / count + EPS)


def call(body, outs, *ins, smem=0, mib=10):
    specs = [pl.BlockSpec(memory_space=pltpu.SMEM)] * smem + [pl.BlockSpec(memory_space=pltpu.VMEM)] * (len(ins) - smem)
    return pl.pallas_call(
        body,
        out_shape=[jax.ShapeDtypeStruct(s, f32) for s in outs],
        in_specs=specs,
        out_specs=[pl.BlockSpec(memory_space=pltpu.VMEM)] * len(outs),
        compiler_params=pltpu.CompilerParams(vmem_limit_bytes=mib * 1024 * 1024),
    )(*ins)


def chosen(rows, lanes, kind, start=0):
    r = lax.broadcasted_iota(jnp.int32, (rows, lanes), 0)
    n = lax.broadcasted_iota(jnp.int32, (rows, lanes), 1)
    n = n // 32 + start if kind == "h" else n % 32
    return jnp.where(r == n, 1.0, 0.0).astype(f32)


def expanded(ec_t, lanes, start=0):
    ce = dg(ec_t[:, :32], chosen(32, lanes, "v"), 1, 0, FULL)
    ee = dg(ec_t[:8, 32:64], chosen(32, lanes, "h", start), 1, 0, FULL)
    return ee, ce, (ee[:, None, :] * ce[None, :, :]).reshape(128, lanes)


def residual_body(first, *refs):
    if first:
        third_ref, c_ref, b_ref, x1_ref, gb_ref, obs_ref, ec_ref = refs
        for l in range(2):
            for t in range(8):
                obs_ref[l, :, 128 * t : 128 * t + 128] = third_ref[2 * t + l, :48, :]
        ec_t = c_ref[...]
        e_sum = third_ref[0, 64:72, :]
        for t in range(1, 8):
            e_sum = e_sum + third_ref[2 * t, 64:72, :]
        ec_t = ec_t + jnp.concatenate([e_sum, jnp.zeros_like(e_sum)], axis=0)
        ec_ref[...] = ec_t
        w = [third_ref[:, 48 + 8 * l : 56 + 8 * l, :].reshape(128, 128) for l in range(2)]
    else:
        w_ref, ec_ref, b_ref, obs_ref, x1_ref, gb_ref = refs
        ec_t = ec_ref[...]
        w = [w_ref[:, 8 * l : 8 * l + 8, :].reshape(128, 128) for l in range(2)]
    ee, ce, ec = expanded(ec_t, 1024)
    b = b_ref[...]
    bt = b.T
    gb, x = None, None
    x1_ref[:, 16:24, :] = jnp.zeros((16, 8, 128), f32)
    for l in range(2):
        q = dg(w[l].T, ec, 1, 0)
        res = SCALE * dg(b, q, 1, 0) - obs_ref[l]
        gb_l = dg(res, q, 1, 1)
        gb = gb_l if gb is None else gb + gb_l
        up = SCALE * dg(bt, res, 1, 0)
        x1_ref[:, 8 * l : 8 * l + 8, :] = dg(ec, up, 1, 1).reshape(16, 8, 128)
        x_l = dg(w[l], up, 1, 0)
        x = x_l if x is None else x + x_l
    gb_ref[...] = SCALE * gb
    x = x.reshape(8, 16, 1024)
    ge = dg(jnp.sum(x * ce[None], axis=1), chosen(32, 1024, "h"), 1, 1, FULL)
    gc = dg(jnp.sum(x * ee[:, None], axis=0), chosen(32, 1024, "v"), 1, 1, FULL)
    for r in range(16):
        x1_ref[r, 16:17, 0:32] = gc[r : r + 1]
        if r < 8:
            x1_ref[r, 16:17, 32:64] = ge[r : r + 1]


def products(a_ref, far, core):
    a_two = jnp.concatenate([a_ref[pl.ds(far, 1), :], a_ref[pl.ds(far + 32, 1), :]], axis=0)
    top, low = [], []
    for g in core:
        w = dg(a_two, g, 1, 1)
        top.append(w[0:1])
        low.append(w[1:2])
    return jnp.concatenate(top + low, axis=0)


def near_sum_body(x1_ref, gb_ref, core_ref, x2_ref, ga_ref):
    s = jnp.sum(x1_ref[...], axis=0)
    acc = None
    for c in range(8):
        p = jnp.concatenate([s[c : c + 1], s[8 + c : 9 + c]], axis=0)
        t = dg(p, core_ref[c], 1, 0)
        acc = t if acc is None else acc + t
    ga_ref[...] = jnp.concatenate([acc[:, :128], acc[:, 128:], jnp.zeros((4, 128), f32)], axis=0)
    tail = jnp.concatenate([jnp.zeros((2, 128), f32), s[16:17], jnp.zeros((5, 128), f32)], axis=0)
    x2_ref[...] = jnp.broadcast_to(jnp.concatenate([s[:16], tail], axis=0)[None], (32, 24, 128))
    for k in range(24):
        x2_ref[k, 16:18, :] = gb_ref[2 * k : 2 * k + 2, :]


def core_grad_body(x2_ref, a_ref, ga_ref, x3_ref, g_ref, gb_ref):
    a = a_ref[...]
    sq = jnp.zeros((1, 128), f32)
    for c in range(8):
        p = jnp.concatenate([x2_ref[:, c, :], x2_ref[:, 8 + c, :]], axis=0)
        g = dg(p.T, a, 1, 0)
        g_ref[c] = g
        s = jnp.sum(g * g, axis=0, keepdims=True)
        sq = sq + s[:, :128] + s[:, 128:]
    s = jnp.sum(x2_ref[:, 16:24, :], axis=0)
    gb_ref[...] = s
    gb = s[0:2]
    rows = jnp.concatenate(
        [ga_ref[0:4], s[2:3], sq, jnp.sum(gb * gb, axis=0, keepdims=True), jnp.zeros((1, 128), f32)], axis=0
    )
    x3_ref[...] = jnp.broadcast_to(rows[None], (16, 8, 128))


def near_update_body(x3_ref, gb_ref, ec_ref, x4_ref, new_ref, sq_ref):
    s = jnp.sum(x3_ref[...], axis=0)
    g = x3_ref[:, 4, :]
    lane = lax.broadcasted_iota(jnp.int32, (16, 128), 1)
    gc = jnp.where(lane < 32, g, 0.0)
    ge = jnp.where(jnp.logical_and(lane >= 32, lane < 64), g, 0.0)
    new_ref[...] = ec_ref[...] - rate(jnp.sum(gc * gc), 512.0) * gc - rate(jnp.sum(ge * ge), 256.0) * ge
    sq_ref[...] = jnp.broadcast_to(jnp.sum(s[5:6], axis=1, keepdims=True), (8, 128))
    rows = jnp.concatenate([s[0:4], gb_ref[0:2], s[6:7], jnp.zeros((1, 128), f32)], axis=0)
    x4_ref[...] = jnp.broadcast_to(rows[None], (32, 8, 128))


def far_update_body(last, far_ref, x4_ref, a_ref, b_ref, core_ref, g_ref, sq_ref, x5_ref, a_new, *rest):
    ga = jnp.concatenate(
        [
            jnp.concatenate([x4_ref[:, 0, :], x4_ref[:, 1, :]], axis=0),
            jnp.concatenate([x4_ref[:, 2, :], x4_ref[:, 3, :]], axis=0),
        ],
        axis=1,
    )
    a_new[...] = a_ref[...] - rate(jnp.sum(ga * ga), 16384.0) * ga
    rb = rate(jnp.sum(x4_ref[:, 6, :]), 98304.0)
    gb = jnp.concatenate([x4_ref[k, 4:6, :] for k in range(24)], axis=0)
    b_new = b_ref[...] - rb * gb
    far = far_ref[0]
    rg = ETA * lax.rsqrt(sq_ref[0:1, 0:1] * (1.0 / 4194304) + EPS)
    core = [core_ref[c] - rg * g_ref[c] for c in range(8)]
    x5_ref[:, 0:16, :] = jnp.broadcast_to(products(a_new, far, core)[None], (16, 16, 128))
    if not last:
        b_out, core_out = rest
        b_out[...] = b_new
        for c in range(8):
            core_out[c] = core[c]
        return
    x5_ref[:, 16:64, :] = jnp.broadcast_to(b_new[None], (16, 48, 128))
    at = pl.ds(pl.multiple_of(far // 2 * 8, 8), 8)
    own = [[], []]
    for c in range(8):
        v = core_ref[c, at, :] - rg * g_ref[c, at, :]
        v = jnp.where(far % 2 == 0, v[0:4], v[4:8])
        for co in range(2):
            own[co] += [v[2 * co : 2 * co + 2, :128], v[2 * co : 2 * co + 2, 128:]]
    for co in range(2):
        rows = jnp.concatenate(own[co], axis=0)
        for t in range(8):
            x5_ref[2 * t + co, 64:96, :] = rows


def pack_body(tm_ref, core_ref, a_ref, out_ref):
    rows = core_ref[tm_ref[0]]
    for k in range(2):
        out_ref[k, 0:32, :] = rows[32 * k : 32 * k + 32]
        out_ref[k, 32:34, :] = a_ref[...]
        out_ref[k, 34:40, :] = jnp.zeros((6, 128), f32)


def spread_body(first_ref, out_ref):
    parts = []
    for k in range(16):
        parts += [first_ref[co, 2 * k : 2 * k + 2, :] for co in range(2)]
    for half in range(2):
        parts += [first_ref[l, 32 + half : 33 + half, :] for l in range(2)]
    parts.append(jnp.zeros((4, 128), f32))
    rows = jnp.concatenate(parts, axis=0)
    out_ref[...] = jnp.broadcast_to(rows[None], (32, 72, 128))


def first_products_body(far_ref, second_ref, obs_ref, e_ref, third_ref, core_ref, a_ref):
    for k in range(32):
        for c in range(8):
            for half in range(2):
                r = 4 * (2 * c + half)
                core_ref[c, 4 * k : 4 * k + 4, 128 * half : 128 * half + 128] = second_ref[k, r : r + 4, :]
    for half in range(2):
        for l in range(2):
            a_ref[32 * l : 32 * l + 32, 128 * half : 128 * half + 128] = second_ref[:, 64 + 2 * half + l, :]
    x = jnp.concatenate([products(a_ref, far_ref[0], [core_ref[c] for c in range(8)]), e_ref[...]], axis=0)
    third_ref[:, 48:72, :] = jnp.broadcast_to(x[None], (16, 24, 128))
    obs_t = jnp.concatenate([obs_ref[pl.ds(j, 128, stride=6), :].T for j in range(6)], axis=0)
    third_ref[:, 0:48, :] = obs_t.reshape(16, 48, 128)


def final_body(idx_ref, x5_ref, ec_ref, obs_ref, res_ref, b_ref, core_ref):
    tm, co = idx_ref[0], idx_ref[1]
    _, _, ec = expanded(ec_ref[...], 128, 4 * tm)
    w = x5_ref[:, pl.ds(pl.multiple_of(co * 8, 8), 8), :].reshape(128, 128)
    b = x5_ref[:, 16:64, :].reshape(768, 128)
    b_ref[...] = b
    core_ref[...] = x5_ref[:, 64:96, :].reshape(512, 128)
    q = dg(ec.T, w, 1, 0)
    for j in range(6):
        at = pl.ds(j, 128, stride=6)
        res_ref[at, :] = SCALE * dg(q, b[128 * j : 128 * j + 128], 1, 1) - obs_ref[at, :]


def shards(observations, a_factor, b_factor, c_factor, e_factor, core):
    tm = lax.axis_index("zl") * 4 + lax.axis_index("x")
    co = lax.axis_index("co")
    far = lax.axis_index("y") * 4 + lax.axis_index("zh")
    near = tm * 2 + co
    far_i = far.astype(jnp.int32).reshape(1)

    rows = core.reshape(8, 16, 2, 2, 128).transpose(0, 1, 3, 2, 4).reshape(8, 64, 128)
    (first,) = call(pack_body, [(2, 40, 128)], tm.astype(jnp.int32).reshape(1), rows, a_factor.reshape(2, 128), smem=1)
    (second,) = call(spread_body, [(32, 72, 128)], swap(first, "co"))
    obs = observations.reshape(768, 128)
    e_own = lax.dynamic_update_slice(jnp.zeros((8, 128), f32), e_factor.T, (0, 32 + 4 * tm))
    third, core_part, a_all = call(
        first_products_body, [(16, 72, 128), (8, 128, 256), (64, 256)], far_i, swap(second, FAR), obs, e_own, smem=1
    )
    third = swap(third, NEAR)
    b_part = lax.dynamic_slice_in_dim(b_factor, near * 48, 48, 0)
    c_t = jnp.pad(c_factor.T, ((0, 0), (0, 96)))

    for step in range(STEPS):
        if step == 0:
            x1, gb, obs_part, ec_t = call(
                functools.partial(residual_body, True),
                [(16, 24, 128), (48, 128), (2, 48, 1024), (16, 128)],
                third, c_t, b_part, mib=16,
            )
        else:
            x1, gb = call(
                functools.partial(residual_body, False), [(16, 24, 128), (48, 128)], x5, ec_t, b_part, obs_part, mib=16
            )
        x2, ga = call(near_sum_body, [(32, 24, 128), (8, 128)], swap(x1, NEAR), gb, core_part)
        x3, g_core, gb = call(core_grad_body, [(16, 8, 128), (8, 128, 256), (8, 128)], swap(x2, FAR), a_all, ga)
        x4, ec_t, sq = call(near_update_body, [(32, 8, 128), (16, 128), (8, 128)], swap(x3, NEAR), gb, ec_t)
        last = step == STEPS - 1
        more = [] if last else [(48, 128), (8, 128, 256)]
        x5, a_all, *rest = call(
            functools.partial(far_update_body, last),
            [(16, 96 if last else 16, 128), (64, 256)] + more,
            far_i, swap(x4, FAR), a_all, b_part, core_part, g_core, sq,
            smem=1,
        )
        x5 = swap(x5, NEAR)
        if not last:
            b_part, core_part = rest

    idx = jnp.stack([tm, co]).astype(jnp.int32)
    residual, b_new, core_new = call(
        final_body, [(768, 128), (768, 128), (512, 128)], idx, x5, ec_t, obs, smem=1
    )
    core_new = core_new.reshape(8, 16, 2, 2, 128).transpose(0, 1, 3, 2, 4).reshape(8, 16, 2, 256)
    a_new = lax.dynamic_slice_in_dim(a_all, co * 32 + far, 1, 0)
    e_new = lax.dynamic_slice(ec_t, (0, 32 + 4 * tm), (8, 4)).T
    return (residual.reshape(4, 32, 1, 768), a_new, b_new, ec_t[:, :32].T, e_new, core_new)


def solution(mesh):
    fine = Mesh(mesh.devices.reshape(8, 4, 2, 2, 4), ("y", "zh", "co", "zl", "x"))
    grid, tm = ("y", "zh", "co"), ("zl", "x")
    specs = (P(tm, None, grid, None), P(grid, None), P(), P(), P(tm, None), P(None, None, grid, None))
    return jax.shard_map(shards, mesh=fine, in_specs=specs, out_specs=specs, check_vma=False)
```

```python
import functools

import jax
import jax.numpy as jnp
from jax import lax
from jax.experimental import pallas as pl
from jax.experimental.pallas import tpu as pltpu
from jax.sharding import Mesh, PartitionSpec as P

STEPS = 2
ETA = 0.2
EPS = 1e-06
SCALE = float(256 * 128 * 16 * 8) ** (-0.5)

FAR = ("y", "zh")
NEAR = ("zl", "x", "co")
NF, NN = 32, 16
PACK_MIB = 56
HIGH, FULL = lax.Precision.HIGH, lax.Precision.HIGHEST
f32 = jnp.float32


def swap(x, axes):
    return lax.all_to_all(x, axes, 0, 0, tiled=True)


def dg(a, b, ca, cb, precision=HIGH):
    return lax.dot_general(a, b, (((ca,), (cb,)), ((), ())), precision=precision, preferred_element_type=f32)


def rate(total, count):
    return ETA * lax.rsqrt(total / count + EPS)


def call(body, outs, *ins, smem=0, hbm=0, scratch=(), mib=10):
    spaces = [pltpu.SMEM] * smem + [pltpu.HBM] * hbm + [pltpu.VMEM] * (len(ins) - smem - hbm)
    specs = [pl.BlockSpec(memory_space=space) for space in spaces]
    return pl.pallas_call(
        body,
        out_shape=[jax.ShapeDtypeStruct(s, f32) for s in outs],
        in_specs=specs,
        out_specs=[pl.BlockSpec(memory_space=pltpu.VMEM)] * len(outs),
        scratch_shapes=list(scratch),
        compiler_params=pltpu.CompilerParams(vmem_limit_bytes=mib * 1024 * 1024),
    )(*ins)


def chosen(rows, lanes, kind, start=0):
    r = lax.broadcasted_iota(jnp.int32, (rows, lanes), 0)
    n = lax.broadcasted_iota(jnp.int32, (rows, lanes), 1)
    n = n // 32 + start if kind == "h" else n % 32
    return jnp.where(r == n, 1.0, 0.0).astype(f32)


def hour_lanes(tm):
    r = lax.broadcasted_iota(jnp.int32, (4, 128), 0)
    n = lax.broadcasted_iota(jnp.int32, (4, 128), 1)
    return jnp.where(n == r + 32 + 4 * tm, 1.0, 0.0).astype(f32)


def expanded(ec_t, lanes, start=0):
    ce = dg(ec_t[:, :32], chosen(32, lanes, "v"), 1, 0, FULL)
    ee = dg(ec_t[:8, 32:64], chosen(32, lanes, "h", start), 1, 0, FULL)
    return ee, ce, (ee[:, None, :] * ce[None, :, :]).reshape(128, lanes)


def residual_body(first, tm_ref, *refs):
    tm = tm_ref[0]
    if first:
        near_ref, b_ref, w_ref, obs_ref, c_ref, e_ref, x1_ref, own_ref, ec_out = refs
        b = b_ref[...]
        own_ref[...] = b_ref[pl.ds(pl.multiple_of(48 * near_ref[0], 8), 48), :]
        e = dg(e_ref[...], hour_lanes(tm), 0, 0, FULL)
        ec_out[...] = jnp.concatenate([e, jnp.zeros((8, 128), f32)], axis=0)
        ec_out[:, 0:32] = c_ref[...]
        ec_t = ec_out[...]
    else:
        w_ref, obs_ref, ec_ref, x1_ref = refs
        b = w_ref[:, 8:56, :].reshape(768, 128)
        ec_t = ec_ref[...]
    w = w_ref[:, 0:8, :].reshape(128, 128)
    ee, ce, ec = expanded(ec_t, 128, 4 * tm)
    q = dg(ec.T, w, 1, 0)
    obs = jnp.concatenate([obs_ref[pl.ds(j, 128, stride=6), :] for j in range(6)], axis=1)
    res = SCALE * dg(q, b, 1, 1) - obs
    x1_ref[:, 16:64, :] = (SCALE * dg(res.T, q, 1, 0)).reshape(16, 48, 128)
    up = SCALE * dg(res, b, 1, 0)
    x1_ref[:, 0:8, :] = dg(ec, up, 1, 0).reshape(16, 8, 128)
    x = dg(w, up, 1, 1).reshape(8, 16, 128)
    ge = dg(jnp.sum(x * ce[None], axis=1), chosen(32, 128, "h", 4 * tm), 1, 1, FULL)
    gc = dg(jnp.sum(x * ee[:, None], axis=0), chosen(32, 128, "v"), 1, 1, FULL)
    x1_ref[:, 8:16, :] = jnp.zeros((16, 8, 128), f32)
    for r in range(16):
        x1_ref[r, 8:9, 0:32] = gc[r : r + 1]
        if r < 8:
            x1_ref[r, 8:9, 32:64] = ge[r : r + 1]


def products(a_ref, far, core):
    a_two = jnp.concatenate([a_ref[pl.ds(far, 1), :], a_ref[pl.ds(far + 32, 1), :]], axis=0)
    top, low = [], []
    for g in core:
        w = dg(a_two, g, 1, 1)
        top.append(w[0:1])
        low.append(w[1:2])
    return jnp.concatenate(top + low, axis=0)


def near_sum_body(x1_ref, core_ref, x2_ref, ga_ref):
    p = []
    for l in range(2):
        t = x1_ref[l, 0:8, :]
        for k in range(1, 8):
            t = t + x1_ref[2 * k + l, 0:8, :]
        p.append(t)
    s = jnp.sum(x1_ref[:, 8:16, :], axis=0)
    gb = jnp.sum(x1_ref[:, 16:64, :], axis=0)
    s = jnp.concatenate(p + [jnp.zeros((8, 128), f32), s], axis=0)
    acc = None
    for c in range(8):
        p = jnp.concatenate([s[c : c + 1], s[8 + c : 9 + c]], axis=0)
        x2_ref[:, :, 128 * c : 128 * c + 128] = jnp.broadcast_to(p[None], (32, 2, 128))
        t = dg(p, core_ref[c], 1, 0)
        acc = t if acc is None else acc + t
    ga_ref[...] = jnp.concatenate([acc[:, :128], acc[:, 128:], jnp.zeros((4, 128), f32)], axis=0)
    tail = jnp.concatenate([s[24:25], jnp.zeros((1, 128), f32)], axis=0)
    x2_ref[:, :, 1152:1280] = jnp.broadcast_to(tail[None], (32, 2, 128))
    x2_ref[:, :, 1024:1152] = jnp.zeros((32, 2, 128), f32)
    for k in range(24):
        x2_ref[k, :, 1024:1152] = gb[2 * k : 2 * k + 2]


def core_grad_body(x2_ref, a_ref, ga_ref, x3_ref, g_ref, gb_ref):
    a = a_ref[...]
    sq = jnp.zeros((1, 128), f32)
    for c in range(8):
        p = jnp.concatenate([x2_ref[:, l, 128 * c : 128 * c + 128] for l in range(2)], axis=0)
        g = dg(p.T, a, 1, 0)
        g_ref[c] = g
        s = jnp.sum(g * g, axis=0, keepdims=True)
        sq = sq + s[:, :128] + s[:, 128:]
    gb = jnp.sum(x2_ref[:, :, 1024:1152], axis=0)
    s = jnp.sum(x2_ref[:, :, 1152:1280], axis=0)
    gb_ref[...] = jnp.concatenate([gb, jnp.zeros((6, 128), f32)], axis=0)
    rows = jnp.concatenate(
        [ga_ref[0:4], s[0:1], sq, jnp.sum(gb * gb, axis=0, keepdims=True), jnp.zeros((1, 128), f32)], axis=0
    )
    x3_ref[...] = jnp.broadcast_to(rows[None], (16, 8, 128))


def near_update_body(x3_ref, gb_ref, ec_ref, x4_ref, new_ref, sq_ref):
    s = jnp.sum(x3_ref[...], axis=0)
    g = x3_ref[:, 4, :]
    lane = lax.broadcasted_iota(jnp.int32, (16, 128), 1)
    gc = jnp.where(lane < 32, g, 0.0)
    ge = jnp.where(jnp.logical_and(lane >= 32, lane < 64), g, 0.0)
    new_ref[...] = ec_ref[...] - rate(jnp.sum(gc * gc), 512.0) * gc - rate(jnp.sum(ge * ge), 256.0) * ge
    sq_ref[...] = jnp.broadcast_to(jnp.sum(s[5:6], axis=1, keepdims=True), (8, 128))
    rows = jnp.concatenate([s[0:4], gb_ref[0:2], s[6:7], jnp.zeros((1, 128), f32)], axis=0)
    x4_ref[...] = jnp.broadcast_to(rows[None], (32, 8, 128))


def far_update_body(last, far_ref, x4_ref, a_ref, b_ref, core_ref, g_ref, sq_ref, x5_ref, a_new, *rest):
    ga = jnp.concatenate(
        [
            jnp.concatenate([x4_ref[:, 0, :], x4_ref[:, 1, :]], axis=0),
            jnp.concatenate([x4_ref[:, 2, :], x4_ref[:, 3, :]], axis=0),
        ],
        axis=1,
    )
    a_new[...] = a_ref[...] - rate(jnp.sum(ga * ga), 16384.0) * ga
    rb = rate(jnp.sum(x4_ref[:, 6, :]), 98304.0)
    gb = jnp.concatenate([x4_ref[k, 4:6, :] for k in range(24)], axis=0)
    b_new = b_ref[...] - rb * gb
    far = far_ref[0]
    rg = ETA * lax.rsqrt(sq_ref[0:1, 0:1] * (1.0 / 4194304) + EPS)
    core = [core_ref[c] - rg * g_ref[c] for c in range(8)]
    w = products(a_new, far, core)
    for k in range(16):
        x5_ref[k, 0:8, :] = w[8 * (k % 2) : 8 * (k % 2) + 8]
    x5_ref[:, 8:56, :] = jnp.broadcast_to(b_new[None], (16, 48, 128))
    if not last:
        b_out, core_out = rest
        b_out[...] = b_new
        for c in range(8):
            core_out[c] = core[c]
        return
    at = pl.ds(pl.multiple_of(far // 2 * 8, 8), 8)
    own = [[], []]
    for c in range(8):
        v = core_ref[c, at, :] - rg * g_ref[c, at, :]
        v = jnp.where(far % 2 == 0, v[0:4], v[4:8])
        for co in range(2):
            own[co] += [v[2 * co : 2 * co + 2, :128], v[2 * co : 2 * co + 2, 128:]]
    for co in range(2):
        rows = jnp.concatenate(own[co], axis=0)
        for t in range(8):
            x5_ref[2 * t + co, 56:88, :] = rows


def pack_body(tm_ref, core_hbm, a_hbm, out_ref, core_ref, a_ref, sems):
    copies = [
        pltpu.make_async_copy(core_hbm.at[tm_ref[0]], core_ref, sems.at[0]),
        pltpu.make_async_copy(a_hbm, a_ref, sems.at[1]),
    ]
    for copy in copies:
        copy.start()
    for copy in copies:
        copy.wait()
    for co in range(2):
        for j in range(16):
            at = 32 * co + 2 * j
            rows = jnp.broadcast_to(core_ref[at : at + 2, :][None], (32, 2, 128))
            for k in range(32):
                out_ref[2 * k + co, :, 128 * j : 128 * j + 128] = rows[k]
    out_ref[:, :, 2048:2176] = jnp.broadcast_to(a_ref[...][None], (64, 2, 128))


def first_products_body(far_ref, all_ref, x5_ref, core_ref, a_ref):
    for k in range(64):
        for c in range(8):
            core_ref[c, 2 * k : 2 * k + 2, :] = all_ref[k, :, 256 * c : 256 * c + 256]
        for half in range(2):
            at = 32 * (k % 2) + k // 2
            lanes = slice(128 * half, 128 * half + 128)
            a_ref[at : at + 1, lanes] = all_ref[k, half : half + 1, 2048:2176]
    x = products(a_ref, far_ref[0], [core_ref[c] for c in range(8)])
    for k in range(16):
        x5_ref[k] = x[8 * (k % 2) : 8 * (k % 2) + 8]


def final_body(
    tm_ref, co_ref, far_ref, obs_ref, x5_ref, ec_ref, a_ref,
    res_ref, b_ref, core_ref, a_out, c_out, e_out,
):
    tm, co = tm_ref[0], co_ref[0]
    ec_t = ec_ref[...]
    _, _, ec = expanded(ec_t, 128, 4 * tm)
    w = x5_ref[:, 0:8, :].reshape(128, 128)
    b = x5_ref[:, 8:56, :].reshape(768, 128)
    b_ref[...] = b
    core_ref[...] = x5_ref[:, 56:88, :].reshape(512, 128)
    q = dg(ec.T, w, 1, 0)
    for j in range(6):
        at = pl.ds(j, 128, stride=6)
        res_ref[at, :] = SCALE * dg(q, b[128 * j : 128 * j + 128], 1, 1) - obs_ref[at, :]
    a_out[...] = a_ref[pl.ds(far_ref[0] + 32 * co, 1), :]
    c_out[...] = ec_t[:, 0:32]
    e_out[...] = dg(hour_lanes(tm), ec_t[0:8], 1, 1, FULL)


def shards(observations, a_factor, b_factor, c_factor, e_factor, core):
    tm = (lax.axis_index("zl") * 4 + lax.axis_index("x")).astype(jnp.int32).reshape(1)
    co = lax.axis_index("co").astype(jnp.int32).reshape(1)
    far = (lax.axis_index("y") * 4 + lax.axis_index("zh")).astype(jnp.int32).reshape(1)

    near = 2 * tm + co

    rows = core.reshape(8, 16, 2, 2, 128).transpose(0, 1, 3, 2, 4).reshape(8, 64, 128)
    obs = observations.reshape(768, 128)
    (first,) = call(
        pack_body,
        [(64, 2, 2176)],
        tm, rows, a_factor.reshape(2, 128),
        smem=1, hbm=2, mib=PACK_MIB,
        scratch=(pltpu.VMEM((64, 128), f32), pltpu.VMEM((2, 128), f32), pltpu.SemaphoreType.DMA((2,))),
    )
    x5, core_part, a_all = call(
        first_products_body,
        [(16, 8, 128), (8, 128, 256), (64, 256)],
        far, swap(first, FAR + ("co",)),
        smem=1,
    )
    x5 = swap(x5, NEAR)

    for step in range(STEPS):
        last = step == STEPS - 1
        if step == 0:
            x1, b_part, ec_t = call(
                functools.partial(residual_body, True),
                [(16, 64, 128), (48, 128), (16, 128)],
                tm, near, b_factor, x5, obs, c_factor.T, e_factor,
                smem=2,
            )
        else:
            (x1,) = call(functools.partial(residual_body, False), [(16, 64, 128)], tm, x5, obs, ec_t, smem=1)
        x2, ga = call(near_sum_body, [(32, 2, 1280), (8, 128)], swap(x1, NEAR), core_part)
        x3, g_core, gb = call(core_grad_body, [(16, 8, 128), (8, 128, 256), (8, 128)], swap(x2, FAR), a_all, ga)
        x4, ec_t, sq = call(near_update_body, [(32, 8, 128), (16, 128), (8, 128)], swap(x3, NEAR), gb, ec_t)
        more = [] if last else [(48, 128), (8, 128, 256)]
        x5, a_all, *rest = call(
            functools.partial(far_update_body, last),
            [(16, 88 if last else 56, 128), (64, 256)] + more,
            far, swap(x4, FAR), a_all, b_part, core_part, g_core, sq,
            smem=1,
        )
        x5 = swap(x5, NEAR)
        if not last:
            b_part, core_part = rest

    residual, b_new, core_new, a_new, c_new, e_new = call(
        final_body,
        [(768, 128), (768, 128), (512, 128), (1, 256), (16, 32), (4, 8)],
        tm, co, far, obs, x5, ec_t, a_all,
        smem=3,
    )
    core_new = core_new.reshape(8, 16, 2, 2, 128).transpose(0, 1, 3, 2, 4).reshape(8, 16, 2, 256)
    return (residual.reshape(4, 32, 1, 768), a_new, b_new, c_new.T, e_new, core_new)


def solution(mesh):
    fine = Mesh(mesh.devices.reshape(8, 4, 2, 2, 4), ("y", "zh", "co", "zl", "x"))
    grid, tm = ("y", "zh", "co"), ("zl", "x")
    specs = (P(tm, None, grid, None), P(grid, None), P(), P(), P(tm, None), P(None, None, grid, None))
    return jax.shard_map(shards, mesh=fine, in_specs=specs, out_specs=specs, check_vma=False)
```

```python
import functools

import jax
import jax.numpy as jnp
from jax import lax
from jax.experimental import pallas as pl
from jax.experimental.pallas import tpu as pltpu
from jax.sharding import Mesh, PartitionSpec as P

STEPS = 2
ETA = 0.2
EPS = 1e-06
SCALE = float(256 * 128 * 16 * 8) ** (-0.5)

FAR = ("y", "zh")
NEAR = ("zl", "x", "co")
NF, NN = 32, 16
PACK_MIB = 56
HIGH, FULL = lax.Precision.HIGH, lax.Precision.HIGHEST
f32 = jnp.float32


def swap(x, axes):
    return lax.all_to_all(x, axes, 0, 0, tiled=True)


def dg(a, b, ca, cb, precision=HIGH):
    return lax.dot_general(a, b, (((ca,), (cb,)), ((), ())), precision=precision, preferred_element_type=f32)


def rate(total, count):
    return ETA * lax.rsqrt(total / count + EPS)


def call(body, outs, *ins, smem=0, hbm=0, scratch=(), mib=10):
    spaces = [pltpu.SMEM] * smem + [pltpu.HBM] * hbm + [pltpu.VMEM] * (len(ins) - smem - hbm)
    specs = [pl.BlockSpec(memory_space=space) for space in spaces]
    return pl.pallas_call(
        body,
        out_shape=[jax.ShapeDtypeStruct(s, f32) for s in outs],
        in_specs=specs,
        out_specs=[pl.BlockSpec(memory_space=pltpu.VMEM)] * len(outs),
        scratch_shapes=list(scratch),
        compiler_params=pltpu.CompilerParams(vmem_limit_bytes=mib * 1024 * 1024),
    )(*ins)


def chosen(rows, lanes, kind, start=0):
    r = lax.broadcasted_iota(jnp.int32, (rows, lanes), 0)
    n = lax.broadcasted_iota(jnp.int32, (rows, lanes), 1)
    n = n // 32 + start if kind == "h" else n % 32
    return jnp.where(r == n, 1.0, 0.0).astype(f32)


def hour_lanes(tm):
    r = lax.broadcasted_iota(jnp.int32, (4, 128), 0)
    n = lax.broadcasted_iota(jnp.int32, (4, 128), 1)
    return jnp.where(n == r + 32 + 4 * tm, 1.0, 0.0).astype(f32)


def expanded(ec_t, lanes, start=0):
    ce = dg(ec_t[:, :32], chosen(32, lanes, "v"), 1, 0, FULL)
    ee = dg(ec_t[:8, 32:64], chosen(32, lanes, "h", start), 1, 0, FULL)
    return ee, ce, (ee[:, None, :] * ce[None, :, :]).reshape(128, lanes)


def residual_body(first, tm_ref, *refs):
    tm = tm_ref[0]
    w_ref, obs_ref, ec_ref, *b_ref, x1_ref, gec_ref = refs
    b = b_ref[0][...] if first else w_ref[:, 8:56, :].reshape(768, 128)
    ec_t = ec_ref[...]
    w = w_ref[:, 0:8, :].reshape(128, 128)
    ee, ce, ec = expanded(ec_t, 128, 4 * tm)
    q = dg(ec.T, w, 1, 0)
    obs = jnp.concatenate([obs_ref[pl.ds(j, 128, stride=6), :] for j in range(6)], axis=1)
    res = SCALE * dg(q, b, 1, 1) - obs
    x1_ref[:, 8:56, :] = (SCALE * dg(res.T, q, 1, 0)).reshape(16, 48, 128)
    up = SCALE * dg(res, b, 1, 0)
    x1_ref[:, 0:8, :] = dg(ec, up, 1, 0).reshape(16, 8, 128)
    x = dg(w, up, 1, 1).reshape(8, 16, 128)
    ge = dg(jnp.sum(x * ce[None], axis=1), chosen(32, 128, "h", 4 * tm), 1, 1, FULL)
    gc = dg(jnp.sum(x * ee[:, None], axis=0), chosen(32, 128, "v"), 1, 1, FULL)
    gec_ref[...] = jnp.zeros((16, 128), f32)
    gec_ref[:, 0:32] = gc
    gec_ref[0:8, 32:64] = ge


def products(a_ref, far, core):
    a_two = jnp.concatenate([a_ref[pl.ds(far, 1), :], a_ref[pl.ds(far + 32, 1), :]], axis=0)
    top, low = [], []
    for g in core:
        w = dg(a_two, g, 1, 1)
        top.append(w[0:1])
        low.append(w[1:2])
    return jnp.concatenate(top + low, axis=0)


def near_sum_body(x1_ref, gec_ref, core_ref, x2_ref, ga_ref):
    p = []
    for l in range(2):
        t = x1_ref[l, 0:8, :]
        for k in range(1, 8):
            t = t + x1_ref[2 * k + l, 0:8, :]
        p.append(t)
    gb = jnp.sum(x1_ref[:, 8:56, :], axis=0)
    s = jnp.concatenate(p, axis=0)
    acc = None
    for c in range(8):
        p = jnp.concatenate([s[c : c + 1], s[8 + c : 9 + c]], axis=0)
        x2_ref[:, :, 128 * c : 128 * c + 128] = jnp.broadcast_to(p[None], (32, 2, 128))
        t = dg(p, core_ref[c], 1, 0)
        acc = t if acc is None else acc + t
    ga_ref[...] = jnp.concatenate([acc[:, :128], acc[:, 128:], jnp.zeros((4, 128), f32)], axis=0)
    for k in range(24):
        x2_ref[k, :, 1024:1152] = gb[2 * k : 2 * k + 2]
    for k in range(8):
        x2_ref[24 + k, :, 1024:1152] = gec_ref[2 * k : 2 * k + 2, :]


def core_grad_body(far_ref, x2_ref, a_ref, ga_ref, x3_ref, g_ref, gb_ref):
    a = a_ref[...]
    sq = jnp.zeros((1, 128), f32)
    for c in range(8):
        p = jnp.concatenate([x2_ref[:, l, 128 * c : 128 * c + 128] for l in range(2)], axis=0)
        g = dg(p.T, a, 1, 0)
        g_ref[c] = g
        s = jnp.sum(g * g, axis=0, keepdims=True)
        sq = sq + s[:, :128] + s[:, 128:]
    gb = jnp.sum(x2_ref[:, :, 1024:1152], axis=0)
    gb_ref[...] = jnp.concatenate([gb, jnp.zeros((6, 128), f32)], axis=0)
    sb = jnp.where(far_ref[0] < 24, jnp.sum(gb * gb, axis=0, keepdims=True), 0.0)
    x3_ref[...] = jnp.broadcast_to(jnp.concatenate([ga_ref[0:4], gb, sq, sb], axis=0)[None], (16, 8, 128))


def near_update_body(far_ref, x3_ref, gb_ref, x4_ref, sq_ref):
    s = jnp.sum(x3_ref[...], axis=0)
    sq_ref[...] = jnp.broadcast_to(jnp.sum(s[6:7], axis=1, keepdims=True), (8, 128))
    gb = jnp.where(far_ref[0] < 24, gb_ref[0:2], s[4:6])
    rows = jnp.concatenate([s[0:4], gb, s[7:8], jnp.zeros((1, 128), f32)], axis=0)
    x4_ref[...] = jnp.broadcast_to(rows[None], (32, 8, 128))


def far_update_body(
    last, far_ref, x4_ref, a_ref, b_ref, core_ref, g_ref, sq_ref, ec_ref, x5_ref, a_new, ec_new, *rest
):
    ga = jnp.concatenate(
        [
            jnp.concatenate([x4_ref[:, 0, :], x4_ref[:, 1, :]], axis=0),
            jnp.concatenate([x4_ref[:, 2, :], x4_ref[:, 3, :]], axis=0),
        ],
        axis=1,
    )
    a_new[...] = a_ref[...] - rate(jnp.sum(ga * ga), 16384.0) * ga
    rb = rate(jnp.sum(x4_ref[:, 6, :]), 98304.0)
    gb = jnp.concatenate([x4_ref[k, 4:6, :] for k in range(24)], axis=0)
    b_new = b_ref[...] - rb * gb
    g = jnp.concatenate([x4_ref[24 + k, 4:6, :] for k in range(8)], axis=0)
    lane = lax.broadcasted_iota(jnp.int32, (16, 128), 1)
    gc = jnp.where(lane < 32, g, 0.0)
    ge = jnp.where(jnp.logical_and(lane >= 32, lane < 64), g, 0.0)
    ec_new[...] = ec_ref[...] - rate(jnp.sum(gc * gc), 512.0) * gc - rate(jnp.sum(ge * ge), 256.0) * ge
    far = far_ref[0]
    rg = ETA * lax.rsqrt(sq_ref[0:1, 0:1] * (1.0 / 4194304) + EPS)
    core = [core_ref[c] - rg * g_ref[c] for c in range(8)]
    w = products(a_new, far, core)
    for k in range(16):
        x5_ref[k, 0:8, :] = w[8 * (k % 2) : 8 * (k % 2) + 8]
    x5_ref[:, 8:56, :] = jnp.broadcast_to(b_new[None], (16, 48, 128))
    if not last:
        b_out, core_out = rest
        b_out[...] = b_new
        for c in range(8):
            core_out[c] = core[c]
        return
    at = pl.ds(pl.multiple_of(far // 2 * 8, 8), 8)
    own = [[], []]
    for c in range(8):
        v = core_ref[c, at, :] - rg * g_ref[c, at, :]
        v = jnp.where(far % 2 == 0, v[0:4], v[4:8])
        for co in range(2):
            own[co] += [v[2 * co : 2 * co + 2, :128], v[2 * co : 2 * co + 2, 128:]]
    for co in range(2):
        rows = jnp.concatenate(own[co], axis=0)
        for t in range(8):
            x5_ref[2 * t + co, 56:88, :] = rows


def pack_body(tm_ref, core_hbm, a_hbm, out_ref, core_ref, a_ref, sems):
    copies = [
        pltpu.make_async_copy(core_hbm.at[tm_ref[0]], core_ref, sems.at[0]),
        pltpu.make_async_copy(a_hbm, a_ref, sems.at[1]),
    ]
    for copy in copies:
        copy.start()
    for copy in copies:
        copy.wait()
    for co in range(2):
        for j in range(16):
            at = 32 * co + 2 * j
            rows = jnp.broadcast_to(core_ref[at : at + 2, :][None], (32, 2, 128))
            for k in range(32):
                out_ref[2 * k + co, :, 128 * j : 128 * j + 128] = rows[k]
    out_ref[:, :, 2048:2176] = jnp.broadcast_to(a_ref[...][None], (64, 2, 128))


def first_products_body(
    far_ref, tm_ref, near_ref, all_ref, b_ref, c_ref, e_ref, obs_ref, x5_ref, core_ref, a_ref, own_ref, ec_ref
):
    own_ref[...] = b_ref[pl.ds(pl.multiple_of(48 * near_ref[0], 8), 48), :]
    e = dg(e_ref[...], hour_lanes(tm_ref[0]), 0, 0, FULL)
    ec_ref[...] = jnp.concatenate([e, jnp.zeros((8, 128), f32)], axis=0)
    ec_ref[:, 0:32] = c_ref[...]
    for k in range(64):
        for c in range(8):
            core_ref[c, 2 * k : 2 * k + 2, :] = all_ref[k, :, 256 * c : 256 * c + 256]
        for half in range(2):
            at = 32 * (k % 2) + k // 2
            lanes = slice(128 * half, 128 * half + 128)
            a_ref[at : at + 1, lanes] = all_ref[k, half : half + 1, 2048:2176]
    x = products(a_ref, far_ref[0], [core_ref[c] for c in range(8)])
    for k in range(16):
        x5_ref[k] = x[8 * (k % 2) : 8 * (k % 2) + 8]


def final_body(
    tm_ref, co_ref, far_ref, obs_ref, x5_ref, ec_ref, a_ref,
    res_ref, b_ref, core_ref, a_out, c_out, e_out,
):
    tm, co = tm_ref[0], co_ref[0]
    ec_t = ec_ref[...]
    _, _, ec = expanded(ec_t, 128, 4 * tm)
    w = x5_ref[:, 0:8, :].reshape(128, 128)
    b = x5_ref[:, 8:56, :].reshape(768, 128)
    b_ref[...] = b
    core_ref[...] = x5_ref[:, 56:88, :].reshape(512, 128)
    q = dg(ec.T, w, 1, 0)
    for j in range(6):
        at = pl.ds(j, 128, stride=6)
        res_ref[at, :] = SCALE * dg(q, b[128 * j : 128 * j + 128], 1, 1) - obs_ref[at, :]
    a_out[...] = a_ref[pl.ds(far_ref[0] + 32 * co, 1), :]
    c_out[...] = ec_t[:, 0:32]
    e_out[...] = dg(hour_lanes(tm), ec_t[0:8], 1, 1, FULL)


def shards(observations, a_factor, b_factor, c_factor, e_factor, core):
    tm = (lax.axis_index("zl") * 4 + lax.axis_index("x")).astype(jnp.int32).reshape(1)
    co = lax.axis_index("co").astype(jnp.int32).reshape(1)
    far = (lax.axis_index("y") * 4 + lax.axis_index("zh")).astype(jnp.int32).reshape(1)

    near = 2 * tm + co

    rows = core.reshape(8, 16, 2, 2, 128).transpose(0, 1, 3, 2, 4).reshape(8, 64, 128)
    obs = observations.reshape(768, 128)
    (first,) = call(
        pack_body,
        [(64, 2, 2176)],
        tm, rows, a_factor.reshape(2, 128),
        smem=1, hbm=2, mib=PACK_MIB,
        scratch=(pltpu.VMEM((64, 128), f32), pltpu.VMEM((2, 128), f32), pltpu.SemaphoreType.DMA((2,))),
    )
    x5, core_part, a_all, b_part, ec_t = call(
        first_products_body,
        [(16, 8, 128), (8, 128, 256), (64, 256), (48, 128), (16, 128)],
        far, tm, near, swap(first, FAR + ("co",)), b_factor, c_factor.T, e_factor, obs,
        smem=3,
    )
    x5 = swap(x5, NEAR)

    for step in range(STEPS):
        last = step == STEPS - 1
        begin = [b_factor] if step == 0 else []
        x1, gec = call(
            functools.partial(residual_body, step == 0),
            [(16, 56, 128), (16, 128)],
            tm, x5, obs, ec_t, *begin,
            smem=1,
        )
        x2, ga = call(near_sum_body, [(32, 2, 1152), (8, 128)], swap(x1, NEAR), gec, core_part)
        x3, g_core, gb = call(
            core_grad_body, [(16, 8, 128), (8, 128, 256), (8, 128)], far, swap(x2, FAR), a_all, ga, smem=1
        )
        x4, sq = call(near_update_body, [(32, 8, 128), (8, 128)], far, swap(x3, NEAR), gb, smem=1)
        more = [] if last else [(48, 128), (8, 128, 256)]
        x5, a_all, ec_t, *rest = call(
            functools.partial(far_update_body, last),
            [(16, 88 if last else 56, 128), (64, 256), (16, 128)] + more,
            far, swap(x4, FAR), a_all, b_part, core_part, g_core, sq, ec_t,
            smem=1,
        )
        x5 = swap(x5, NEAR)
        if not last:
            b_part, core_part = rest

    residual, b_new, core_new, a_new, c_new, e_new = call(
        final_body,
        [(768, 128), (768, 128), (512, 128), (1, 256), (16, 32), (4, 8)],
        tm, co, far, obs, x5, ec_t, a_all,
        smem=3,
    )
    core_new = core_new.reshape(8, 16, 2, 2, 128).transpose(0, 1, 3, 2, 4).reshape(8, 16, 2, 256)
    return (residual.reshape(4, 32, 1, 768), a_new, b_new, c_new.T, e_new, core_new)


def solution(mesh):
    fine = Mesh(mesh.devices.reshape(8, 4, 2, 2, 4), ("y", "zh", "co", "zl", "x"))
    grid, tm = ("y", "zh", "co"), ("zl", "x")
    specs = (P(tm, None, grid, None), P(grid, None), P(), P(), P(tm, None), P(None, None, grid, None))
    return jax.shard_map(shards, mesh=fine, in_specs=specs, out_specs=specs, check_vma=False)
```
